32 devices in a mesh: seq: 8 (over y, x, core), dp: 4 (over z).
Axes of the slice: x: 2, y: 2, z: 4, core: 2. Of those that a mesh axis runs over, the one named last changes fastest.
Arguments:
- features: bfloat16 [8, 3072, 768], P('dp', 'seq'), may hold values from -32 to 32
- weight: bfloat16 [5, 768, 768], replicated, may hold values from -0.09375 to 0.09375
- cotangent: bfloat16 [8, 1536, 768], P('dp', 'seq'), may hold values from -6 to 6
Outputs:
- trunk_input: bfloat16 [8, 1536, 768], P('dp', None, 'seq')
- input_grad: bfloat16 [8, 3072, 768], P('dp', 'seq')
- weight_grad: float32 [5, 768, 768], P(None, 'dp', 'seq')
The draws below stay inside these ranges and needn't reach their ends.
All inputs are finite; a program needn't handle non-finite values.
Results may differ from the reference program's by a relative error of at most 0.0027.
Values may be sent and summed in bfloat16 or wider, within the bound.
A program may use at most 128 MiB of HBM per device.

```python
import jax
import jax.numpy as jnp
from jax import lax

C = 768
W = 5
LEN = 3072
POOLED = 1536
BATCH = 8


def draw_features(key, part):
    first, second, third = jax.random.split(key, 3)
    shape = (BATCH, LEN, C)
    base = jax.random.truncated_normal(first, -3.5, 3.5, shape, jnp.float32)
    rows = jnp.exp(jax.random.uniform(second, (BATCH, LEN, 1), jnp.float32, jnp.log(0.3), jnp.log(3.0)))
    columns = jnp.exp(jax.random.uniform(third, (1, 1, C), jnp.float32, jnp.log(0.3), jnp.log(3.0)))
    return (base * rows * columns).astype(jnp.bfloat16)


def raised(drawn, stream_key, source, target, shards_of, factor):
    def block_of(axis_at):
        return (jnp.arange(drawn.shape[axis_at]) // (drawn.shape[axis_at] // shards_of)).reshape((-1,) + (1,) * (drawn.ndim - 1 - axis_at))

    near = jax.random.permutation(stream_key, shards_of)[block_of(target)]
    other_side = (block_of(target) + shards_of // 2) % shards_of
    return jnp.where((block_of(source) == near) | (block_of(source) == other_side), factor * drawn, drawn)


def level_of(stream_key, extent, pieces, least, high):
    def one(position, blocks):
        steps = jax.random.uniform(jax.random.fold_in(jax.random.fold_in(stream_key, 6), position), (blocks,), jnp.float32, least / len(pieces), high / len(pieces))
        return jnp.repeat(jnp.exp(steps), extent[position] // blocks).reshape((-1,) + (1,) * (len(extent) - position - 1))

    gain = one(*pieces[0])
    for cut in pieces[1:]:
        gain = gain * one(*cut)
    return gain


def scatter_about(key, shape, scale, limit, pieces=(), kind=jnp.bfloat16):
    factor_of = level_of(key, shape, pieces, -0.22, 0.18) if pieces else 1.0
    drawn = jax.random.normal(key, shape, jnp.float32) * scale * factor_of
    return jnp.minimum(jnp.maximum(drawn, -limit), limit).astype(kind)


def gaussian_with(stream_key, extent, deviation, most, cuts, heavy, held_as=jnp.bfloat16):
    drawn = deviation * jax.random.normal(stream_key, extent, jnp.float32)
    if cuts:
        drawn = drawn * level_of(stream_key, extent, cuts, -0.22, 0.18)
    return jnp.clip(raised(drawn, jax.random.fold_in(stream_key, 3), *heavy), -most, most).astype(held_as)


def setup_inputs(seed: int = 0) -> dict:
    key_list = jax.random.split(jax.random.key(seed), 4)
    return {
        "features": draw_features(jax.random.fold_in(key_list[3], 71), 0),
        "weight": scatter_about(key_list[1], (W, C, C), (W * C) ** -0.5, 0.09375),
        "cotangent": gaussian_with(key_list[2], (BATCH, POOLED, C), 1.0, 6.0, ((0, 4), (1, 8)), (1, 2, 8, 2.0)),
    }


epsilon = 1e-06
root_half = 0.7071067811865476
inv_root_two_pi = 0.3989422804014327

def gaussian_unit(value):
    return 0.5 * value * (1.0 + jax.scipy.special.erf(value * root_half))

def gaussian_slope(value):
    return 0.5 * (1.0 + jax.scipy.special.erf(value * root_half)) + value * inv_root_two_pi * jnp.exp(-0.5 * value * value)

def one_sequence(pair, weight):
    features, cotangent = pair
    length = features.shape[0]
    taps = weight.shape[0]
    reach = taps // 2
    weights32 = weight.astype(jnp.float32)
    floats = features.astype(jnp.float32)
    inverse = lax.rsqrt(lax.optimization_barrier(jnp.mean(floats * floats, axis=-1, keepdims=True)) + epsilon)
    normed = floats * inverse
    activations = gaussian_unit(normed).astype(jnp.bfloat16)
    padded = jnp.pad(activations, ((reach, reach), (0, 0)))
    window = jnp.stack([padded[offset:offset + length] for offset in range(taps)], axis=1).astype(jnp.float32)
    mixed = jnp.einsum('lki,kio->lo', window, weights32)
    summed = floats + mixed
    pooled = (0.5 * (summed[0::2] + summed[1::2])).astype(jnp.bfloat16)
    upward = 0.5 * jnp.repeat(cotangent.astype(jnp.float32), 2, axis=0)
    branch_grad = upward.astype(jnp.bfloat16)
    padded_grad = jnp.pad(branch_grad, ((reach, reach), (0, 0)))
    grad_window = jnp.stack([padded_grad[offset:offset + length] for offset in range(taps)], axis=1).astype(jnp.float32)
    act_grad = jnp.einsum('lko,kio->li', grad_window, weights32[::-1])
    slope_grad = act_grad * gaussian_slope(normed)
    centred = lax.optimization_barrier(jnp.mean(slope_grad * floats, axis=-1, keepdims=True))
    input_grad = (upward + inverse * slope_grad - floats * inverse ** 3 * centred).astype(jnp.bfloat16)
    kernel_grad = jnp.einsum('lki,lo->kio', window, branch_grad.astype(jnp.float32))
    return (pooled, input_grad, kernel_grad)

def reference(features, weight, cotangent):
    pooled, input_grad, kernel_grad = lax.map(lambda pair: one_sequence(pair, weight), (features, cotangent))
    return (pooled, input_grad, lax.optimization_barrier(jnp.sum(kernel_grad, axis=0)))
```

```python
import functools

import jax
import jax.numpy as jnp
from jax import lax
from jax.experimental import pallas as pl
from jax.experimental.pallas import tpu as pltpu
from jax.sharding import PartitionSpec as P

epsilon = 1e-06
root_half = 0.7071067811865476
inv_root_two_pi = 0.3989422804014327
edge = 16
f32 = jnp.float32
bf16 = jnp.bfloat16


def phases(rows):
    inverse = lax.rsqrt(jnp.mean(rows * rows, axis=-1, keepdims=True) + epsilon)
    normed = rows * inverse
    cdf = 0.5 * (1.0 + lax.erf(normed * root_half))
    slope = cdf + normed * inv_root_two_pi * jnp.exp(-0.5 * normed * normed)
    return normed * cdf, slope * inverse


def kernel(
    n, zs, f_ref, w_ref, g_ref,
    trunk_ref, igrad_ref, wg_ref,
    halo_f, halo_g, acts, acts_sib, gext, gt, gt_sib, tslope, prod, part, recv, own,
    zpart, zrecv, zown, pooled, tpart,
    halo_send, halo_recv, sib_send, sib_recv, x_send, x_recv, z_send, z_recv, t_send, t_recv,
):
    batch, half, wide = f_ref.shape
    chans = wide // 2
    taps = w_ref.shape[0]
    rows = batch * half
    chips = n // 2
    oblk = chans // n
    iblk = chans // zs
    me = lax.axis_index("seq")
    core = lax.rem(me, 2)
    chip = me // 2
    sib = me + 1 - 2 * core
    zme = lax.axis_index("dp")

    barrier = pltpu.get_barrier_semaphore()
    for d in range(1, n):
        pl.semaphore_signal(barrier, inc=1, device_id={"seq": lax.rem(me + d, n)},
                            device_id_type=pl.DeviceIdType.MESH)
    for d in range(1, zs):
        pl.semaphore_signal(barrier, inc=1, device_id={"dp": lax.rem(zme + d, zs)},
                            device_id_type=pl.DeviceIdType.MESH)
    pl.semaphore_wait(barrier, n - 1 + zs - 1)

    def remote(src, dst, ssem, rsem, where):
        return pltpu.make_async_remote_copy(
            src_ref=src, dst_ref=dst, send_sem=ssem, recv_sem=rsem,
            device_id=where, device_id_type=pl.DeviceIdType.MESH)

    right = {"seq": lax.rem(me + 1, n)}
    left = {"seq": lax.rem(me + n - 1, n)}
    halos = []
    for side, (where, start) in enumerate(((right, half - edge), (left, 0))):
        halos.append(remote(f_ref.at[:, pl.ds(start, edge)], halo_f.at[side],
                            halo_send.at[2 * side], halo_recv.at[2 * side], where))
        halos.append(remote(g_ref.at[:, pl.ds(start, edge)], halo_g.at[side],
                            halo_send.at[2 * side + 1], halo_recv.at[2 * side + 1], where))
    for copy in halos:
        copy.start()

    chunk = 32
    per = half // chunk

    @pl.loop(0, batch * per)
    def _(step):
        b = step // per
        r = pl.multiple_of(lax.rem(step, per) * chunk, chunk)
        for p in range(2):
            block = f_ref[b, pl.ds(r, chunk), p * chans : (p + 1) * chans].astype(f32)
            act, slope = phases(block)
            acts[p, pl.ds(pl.multiple_of(b * half + r, chunk), chunk), :] = act.astype(bf16)
            tslope[b, pl.ds(r, chunk), p * chans : (p + 1) * chans] = slope

    to_sib = {"seq": sib}
    send_acts = remote(acts.at[:, pl.ds(0, rows)], acts_sib, sib_send.at[0], sib_recv.at[0], to_sib)
    send_acts.start()

    for copy in halos:
        copy.wait()
    index = lax.broadcasted_iota(jnp.int32, (edge, 1), 0)
    has_left = jnp.where(me > 0, 1.0, 0.0)
    has_right = jnp.where(me < n - 1, 1.0, 0.0)

    def edge_rows(ref, lanes):
        out = jnp.zeros((edge, lanes), f32)
        for b in range(batch):
            low = ref[0, b].astype(f32)[edge - 1 : edge, :] * has_left
            high = ref[1, b].astype(f32)[0:1, :] * has_right
            out = jnp.where(index == b, low, out)
            out = jnp.where(index == batch + b, high, out)
        return out

    hf = edge_rows(halo_f, wide)
    hg = 0.5 * edge_rows(halo_g, chans)
    for p in range(2):
        act, _ = phases(hf[:, p * chans : (p + 1) * chans])
        acts[p, pl.ds(rows, edge), :] = act.astype(bf16)
    gext[pl.ds(rows, edge), :] = hg.astype(bf16)

    spot = lax.broadcasted_iota(jnp.int32, (half, 1), 0)

    def later(block, b, tail):
        return jnp.where(spot == 0, tail[b : b + 1, :], pltpu.roll(block, 1, 0))

    def sooner(block, b, tail):
        return jnp.where(spot == half - 1, tail[batch + b : batch + b + 1, :],
                         pltpu.roll(block, half - 1, 0))

    for b in range(batch):
        g0 = 0.5 * g_ref[b].astype(f32)
        gext[pl.ds(b * half, half), :] = g0.astype(bf16)
        for s, shifted in enumerate((sooner(g0, b, hg), g0, later(g0, b, hg))):
            turned = shifted.T.astype(bf16)
            for o in range(n):
                gt[o % 2, s, b, o // 2] = turned[o * oblk : (o + 1) * oblk, :]
    send_gt = remote(gt.at[1 - core], gt_sib, sib_send.at[1], sib_recv.at[1], to_sib)
    send_gt.start()
    send_acts.wait_recv()
    send_gt.wait_recv()

    def product(s, p, slot):
        for m in range(chips):
            total = jnp.zeros((oblk, chans), f32)
            for b in range(batch):
                total += jnp.dot(gt[core, s, b, m], acts[p, b * half : (b + 1) * half, :],
                                 preferred_element_type=f32)
                total += jnp.dot(gt_sib[s, b, m], acts_sib[p, b * half : (b + 1) * half, :],
                                 preferred_element_type=f32)
            prod[slot, m] = total

    def x_copy(t, d):
        other = lax.rem(chip + d, chips)
        return remote(part.at[t, other], recv.at[t, d - 1], x_send.at[t, d - 1],
                      x_recv.at[t, d - 1], {"seq": 2 * other + core})

    product(0, 0, 0)

    @pl.loop(0, taps)
    def _(t):
        now = lax.rem(t + 1, 2)
        product((t + 1) // 2, lax.rem(t + 1, 2), now)
        for m in range(chips):
            part[t, m] = (prod[0, m] + prod[1, m]).astype(bf16)
        own[t] = prod[0, chip] + prod[1, chip]
        for d in range(1, chips):
            x_copy(t, d).start()

    cols = 256

    @pl.loop(0, chans // cols)
    def _(tile):
        c0 = pl.multiple_of(tile * cols, cols)
        w = [w_ref[k, :, pl.ds(c0, cols)] for k in range(taps)]

        def dots(pairs):
            return sum(jnp.dot(acts[p], w[k], preferred_element_type=f32) for p, k in pairs)

        before = dots(((0, 0), (1, 0), (1, 1)))
        middle = dots(((0, 1), (0, 2), (1, 2), (1, 3)))
        after = dots(((0, 3), (0, 4), (1, 4)))
        for b in range(batch):
            at = slice(b * half, (b + 1) * half)
            total = middle[at] + later(before[at], b, before[rows:]) + sooner(after[at], b, after[rows:])
            total += f_ref[b, :, pl.ds(c0, cols)].astype(f32)
            total += f_ref[b, :, pl.ds(chans + c0, cols)].astype(f32)
            pooled[b, :, pl.ds(c0, cols)] = 0.5 * total

    for b in range(batch):
        whole = pooled[b]
        for o in range(n):
            tpart[o, b] = whole[:, o * oblk : (o + 1) * oblk].astype(bf16)

    def t_copy(d):
        other = lax.rem(me + d, n)
        return remote(tpart.at[other], trunk_ref.at[:, pl.ds(pl.multiple_of(me * half, edge), half)],
                      t_send.at[d - 1], t_recv.at[d - 1], {"seq": other})

    for d in range(1, n):
        t_copy(d).start()
    trunk_ref[:, pl.ds(pl.multiple_of(me * half, edge), half), :] = tpart[me]

    def z_copy(t, d):
        other = lax.rem(zme + d, zs)
        return remote(zpart.at[t, other], zrecv.at[t, d - 1], z_send.at[t, d - 1],
                      z_recv.at[t, d - 1], {"dp": other})

    def collect(t):
        total = own[t]
        for d in range(1, chips):
            x_copy(t, d).wait_recv()
        for d in range(1, chips):
            total += recv[t, d - 1].astype(f32)
        for q in range(zs):
            piece = total[:, q * iblk : (q + 1) * iblk]
            zown[t, q] = piece
            zpart[t, q] = piece.astype(bf16)
        for d in range(1, zs):
            z_copy(t, d).start()

    @pl.loop(0, 2)
    def _(t):
        collect(t)

    @pl.loop(0, chans // cols)
    def _(tile):
        c0 = pl.multiple_of(tile * cols, cols)
        q = [
            lax.dot_general(gext[...], w_ref[k, pl.ds(c0, cols), :], (((1,), (1,)), ((), ())),
                            preferred_element_type=f32)
            for k in range(taps)
        ]
        q01, q12, q23, q34 = q[0] + q[1], q[1] + q[2], q[2] + q[3], q[3] + q[4]
        for b in range(batch):
            at = slice(b * half, (b + 1) * half)
            even = q12[at] + sooner(q[0][at], b, q[0][rows:]) + later(q34[at], b, q34[rows:])
            odd = q23[at] + sooner(q01[at], b, q01[rows:]) + later(q[4][at], b, q[4][rows:])
            tslope[b, :, pl.ds(c0, cols)] = tslope[b, :, pl.ds(c0, cols)] * even
            tslope[b, :, pl.ds(chans + c0, cols)] = tslope[b, :, pl.ds(chans + c0, cols)] * odd

    @pl.loop(0, batch * per)
    def _(step):
        b = step // per
        r = pl.multiple_of(lax.rem(step, per) * chunk, chunk)
        up = 0.5 * g_ref[b, pl.ds(r, chunk), :].astype(f32)
        for p in range(2):
            lanes = slice(p * chans, (p + 1) * chans)
            block = f_ref[b, pl.ds(r, chunk), lanes].astype(f32)
            scaled = tslope[b, pl.ds(r, chunk), lanes]
            inverse = lax.rsqrt(jnp.mean(block * block, axis=-1, keepdims=True) + epsilon)
            centred = jnp.mean(scaled * block, axis=-1, keepdims=True) * inverse * inverse
            igrad_ref[b, pl.ds(r, chunk), lanes] = (up + scaled - block * centred).astype(bf16)

    @pl.loop(2, taps)
    def _(t):
        collect(t)

    @pl.loop(0, taps)
    def _(t):
        total = zown[t, zme]
        for d in range(1, zs):
            z_copy(t, d).wait_recv()
        for d in range(1, zs):
            total += zrecv[t, d - 1].astype(f32)
        wg_ref[t] = total
        for d in range(1, zs):
            z_copy(t, d).wait_send()
        for d in range(1, chips):
            x_copy(t, d).wait_send()

    for d in range(1, n):
        t_copy(d).wait()
    send_acts.wait_send()
    send_gt.wait_send()


def shards(features, weight, cotangent):
    n = lax.axis_size("seq")
    zs = lax.axis_size("dp")
    taps, _, chans = weight.shape
    batch, length, _ = features.shape
    half = length // 2
    rows = batch * half
    chips = n // 2
    oblk = chans // n
    iblk = chans // zs
    paired = features.reshape(batch, half, 2 * chans)
    vmem = pl.BlockSpec(memory_space=pltpu.VMEM)
    dma = pltpu.SemaphoreType.DMA
    trunk, igrad, wg = pl.pallas_call(
        functools.partial(kernel, n, zs),
        out_shape=(
            jax.ShapeDtypeStruct((batch, half * n, oblk), bf16),
            jax.ShapeDtypeStruct((batch, half, 2 * chans), bf16),
            jax.ShapeDtypeStruct((taps, oblk, iblk), f32),
        ),
        in_specs=[vmem] * 3,
        out_specs=(vmem,) * 3,
        scratch_shapes=[
            pltpu.VMEM((2, batch, edge, 2 * chans), bf16),
            pltpu.VMEM((2, batch, edge, chans), bf16),
            pltpu.VMEM((2, rows + edge, chans), bf16),
            pltpu.VMEM((2, rows, chans), bf16),
            pltpu.VMEM((rows + edge, chans), bf16),
            pltpu.VMEM((2, 3, batch, chips, oblk, half), bf16),
            pltpu.VMEM((3, batch, chips, oblk, half), bf16),
            pltpu.VMEM((batch, half, 2 * chans), f32),
            pltpu.VMEM((2, chips, oblk, chans), f32),
            pltpu.VMEM((taps, chips, oblk, chans), bf16),
            pltpu.VMEM((taps, chips - 1, oblk, chans), bf16),
            pltpu.VMEM((taps, oblk, chans), f32),
            pltpu.VMEM((taps, zs, oblk, iblk), bf16),
            pltpu.VMEM((taps, zs - 1, oblk, iblk), bf16),
            pltpu.VMEM((taps, zs, oblk, iblk), f32),
            pltpu.VMEM((batch, half, chans), f32),
            pltpu.VMEM((n, batch, half, oblk), bf16),
            dma((4,)), dma((4,)), dma((2,)), dma((2,)),
            dma((taps, chips - 1)), dma((taps, chips - 1)),
            dma((taps, zs - 1)), dma((taps, zs - 1)),
            dma((n - 1,)), dma((n - 1,)),
        ],
        compiler_params=pltpu.CompilerParams(
            collective_id=0, has_side_effects=True, vmem_limit_bytes=60 * 1024 * 1024
        ),
        cost_estimate=pl.CostEstimate(
            flops=2 * rows * chans * chans * 21, bytes_accessed=12_000_000, transcendentals=4 * rows * chans
        ),
    )(paired, weight, cotangent)
    return trunk, igrad.reshape(batch, length, chans), jnp.swapaxes(wg, 1, 2)


def solution(mesh):
    return jax.shard_map(
        shards,
        mesh=mesh,
        in_specs=(P("dp", "seq", None), P(), P("dp", "seq", None)),
        out_specs=(P("dp", None, "seq"), P("dp", "seq", None), P(None, "dp", "seq")),
        check_vma=False,
    )
```

```python
import functools

import jax
import jax.numpy as jnp
from jax import lax
from jax.experimental import pallas as pl
from jax.experimental.pallas import tpu as pltpu
from jax.sharding import PartitionSpec as P

epsilon = 1e-06
root_half = 0.7071067811865476
inv_root_two_pi = 0.3989422804014327
edge = 16
f32 = jnp.float32
bf16 = jnp.bfloat16


def phases(rows):
    inverse = lax.rsqrt(jnp.mean(rows * rows, axis=-1, keepdims=True) + epsilon)
    normed = rows * inverse
    cdf = 0.5 * (1.0 + lax.erf(normed * root_half))
    slope = cdf + normed * inv_root_two_pi * jnp.exp(-0.5 * normed * normed)
    return normed * cdf, slope * inverse


def kernel(
    n, zs, f_ref, w_hbm, g_ref,
    trunk_ref, igrad_ref, wg_ref,
    w_ref, fd, stage, halo_f, halo_g, acts, acts_sib, gext, gt, gt_sib, tslope, prod, part, recv, part2, recv2, keep, own,
    zpart, zrecv, zown, pooled, tpart,
    w_sem, halo_send, halo_recv, sib_send, sib_recv, x_send, x_recv, y_send, y_recv, z_send, z_recv, t_send, t_recv,
):
    batch, length, chans = f_ref.shape
    half = length // 2
    taps = w_hbm.shape[0]
    rows = batch * half
    chips = n // 2
    oblk = chans // n
    iblk = chans // zs
    me = lax.axis_index("seq")
    core = lax.rem(me, 2)
    chip = me // 2
    sib = me + 1 - 2 * core
    zme = lax.axis_index("dp")

    load = pltpu.make_async_copy(w_hbm, w_ref, w_sem.at[0])
    load.start()
    barrier = pltpu.get_barrier_semaphore()
    for d in range(1, n):
        pl.semaphore_signal(barrier, inc=1, device_id={"seq": lax.rem(me + d, n)},
                            device_id_type=pl.DeviceIdType.MESH)
    for d in range(1, zs):
        pl.semaphore_signal(barrier, inc=1, device_id={"dp": lax.rem(zme + d, zs)},
                            device_id_type=pl.DeviceIdType.MESH)
    pl.semaphore_wait(barrier, n - 1 + zs - 1)

    def remote(src, dst, ssem, rsem, where):
        return pltpu.make_async_remote_copy(
            src_ref=src, dst_ref=dst, send_sem=ssem, recv_sem=rsem,
            device_id=where, device_id_type=pl.DeviceIdType.MESH)

    right = {"seq": lax.rem(me + 1, n)}
    left = {"seq": lax.rem(me + n - 1, n)}
    halos = []
    for side, (where, start_last) in enumerate(((right, True), (left, False))):
        start = half - edge if start_last else 0
        f_start = length - edge if start_last else 0
        halos.append(remote(f_ref.at[:, pl.ds(f_start, edge)], halo_f.at[side],
                            halo_send.at[2 * side], halo_recv.at[2 * side], where))
        halos.append(remote(g_ref.at[:, pl.ds(start, edge)], halo_g.at[side],
                            halo_send.at[2 * side + 1], halo_recv.at[2 * side + 1], where))
    for copy in halos:
        copy.start()

    chunk = 32
    per = half // chunk

    def activate(b):
        @pl.loop(0, per)
        def _(step):
            r = pl.multiple_of(step * chunk, chunk)
            raw = f_ref[b, pl.ds(pl.multiple_of(2 * r, chunk), 2 * chunk), :].astype(f32)
            for c in range(chans // 128):
                stage[c] = raw[:, c * 128 : (c + 1) * 128]
            for p in range(2):
                block = jnp.concatenate(
                    [stage[c, pl.ds(p, chunk, stride=2), :] for c in range(chans // 128)], axis=1)
                act, slope = phases(block)
                fd[b, pl.ds(r, chunk), p * chans : (p + 1) * chans] = block.astype(bf16)
                acts[p, pl.ds(pl.multiple_of(b * half + r, chunk), chunk), :] = act.astype(bf16)
                tslope[b, pl.ds(r, chunk), p * chans : (p + 1) * chans] = slope

    to_sib = {"seq": sib}

    def sib_copy(b):
        at = pl.ds(b * half, half)
        return remote(acts.at[:, at], acts_sib.at[:, at], sib_send.at[b + 1], sib_recv.at[b + 1], to_sib)

    for b in range(batch - 1):
        activate(b)
        sib_copy(b).start()

    for copy in halos:
        copy.wait()
    index = lax.broadcasted_iota(jnp.int32, (edge, 1), 0)
    has_left = jnp.where(me > 0, 1.0, 0.0)
    has_right = jnp.where(me < n - 1, 1.0, 0.0)

    def edge_rows(ref, last, first):
        out = jnp.zeros((edge, chans), f32)
        for b in range(batch):
            low = ref[0, b].astype(f32)[last : last + 1, :] * has_left
            high = ref[1, b].astype(f32)[first : first + 1, :] * has_right
            out = jnp.where(index == b, low, out)
            out = jnp.where(index == batch + b, high, out)
        return out

    hg = 0.5 * edge_rows(halo_g, edge - 1, 0)
    gext[pl.ds(rows, edge), :] = hg.astype(bf16)

    spot = lax.broadcasted_iota(jnp.int32, (half, 1), 0)

    def later(block, b, tail):
        return jnp.where(spot == 0, tail[b : b + 1, :], pltpu.roll(block, 1, 0))

    def sooner(block, b, tail):
        return jnp.where(spot == half - 1, tail[batch + b : batch + b + 1, :],
                         pltpu.roll(block, half - 1, 0))

    for b in range(batch):
        g0 = 0.5 * g_ref[b].astype(f32)
        gext[pl.ds(b * half, half), :] = g0.astype(bf16)
        for s, shifted in enumerate((sooner(g0, b, hg), g0, later(g0, b, hg))):
            turned = shifted.T.astype(bf16)
            for o in range(n):
                gt[o % 2, s, b, o // 2] = turned[o * oblk : (o + 1) * oblk, :]
    send_gt = remote(gt.at[1 - core], gt_sib, sib_send.at[0], sib_recv.at[0], to_sib)
    send_gt.start()
    activate(batch - 1)
    sib_copy(batch - 1).start()
    for p in range(2):
        act, _ = phases(edge_rows(halo_f, edge - 2 + p, p))
        acts[p, pl.ds(rows, edge), :] = act.astype(bf16)
    send_gt.wait_recv()
    for b in range(batch):
        sib_copy(b).wait_recv()

    def product(s, p, slot):
        for m in range(chips):
            total = jnp.zeros((oblk, chans), f32)
            for b in range(batch):
                total += jnp.dot(gt[core, s, b, m], acts[p, b * half : (b + 1) * half, :],
                                 preferred_element_type=f32)
                total += jnp.dot(gt_sib[s, b, m], acts_sib[p, b * half : (b + 1) * half, :],
                                 preferred_element_type=f32)
            prod[slot, m] = total

    square = chips == 4
    hblk = oblk // 2
    x = lax.rem(chip, 2)
    y = chip // 2
    beside = chip + 1 - 2 * x
    beyond = chip + 2 - 4 * y
    across = beside + 2 - 4 * y
    near = ((beside, slice(0, hblk)), (beyond, slice(hblk, oblk)))

    def x_copy(t, d):
        if square:
            return remote(part.at[t, d], recv.at[t, d], x_send.at[t, d], x_recv.at[t, d],
                          {"seq": 2 * near[d][0] + core})
        other = lax.rem(chip + d + 1, chips)
        return remote(part.at[t, other], recv.at[t, d], x_send.at[t, d],
                      x_recv.at[t, d], {"seq": 2 * other + core})

    def y_copy(t, h):
        return remote(part2.at[t, h], recv2.at[t, h], y_send.at[t, h], y_recv.at[t, h],
                      {"seq": 2 * near[1 - h][0] + core})

    firsts = 2 if square else chips - 1

    def tap(t):
        product((t + 1) // 2, lax.rem(t + 1, 2), lax.rem(t + 1, 2))

        def both(m, at=slice(None)):
            return prod[0, m, at] + prod[1, m, at]

        if square:
            for h in range(2):
                at = near[h][1]
                part[t, h, 0] = both(near[h][0], at).astype(bf16)
                part[t, h, 1] = both(across, at).astype(bf16)
                keep[t, h] = both(near[1 - h][0], at)
        else:
            for m in range(chips):
                part[t, m] = both(m).astype(bf16)
        for d in range(firsts):
            x_copy(t, d).start()
        own[t] = both(chip)

    def forward(t):
        if square:
            for h in range(2):
                x_copy(t, h).wait_recv()
                part2[t, h] = (keep[t, h] + recv[t, h, 1].astype(f32)).astype(bf16)
                y_copy(t, h).start()

    product(0, 0, 0)
    tap(0)
    load.wait()

    cols = 256

    @pl.loop(0, chans // cols)
    def _(tile):
        tap(tile + 1)
        c0 = pl.multiple_of(tile * cols, cols)
        w = [w_ref[k, :, pl.ds(c0, cols)] for k in range(taps)]

        def dots(pairs):
            return sum(jnp.dot(acts[p], w[k], preferred_element_type=f32) for p, k in pairs)

        before = dots(((0, 0), (1, 0), (1, 1)))
        middle = dots(((0, 1), (0, 2), (1, 2), (1, 3)))
        after = dots(((0, 3), (0, 4), (1, 4)))
        for b in range(batch):
            at = slice(b * half, (b + 1) * half)
            total = middle[at] + later(before[at], b, before[rows:]) + sooner(after[at], b, after[rows:])
            total += fd[b, :, pl.ds(c0, cols)].astype(f32)
            total += fd[b, :, pl.ds(chans + c0, cols)].astype(f32)
            pooled[b, :, pl.ds(c0, cols)] = 0.5 * total
        forward(tile)

    tiles = chans // cols
    for t in range(tiles + 1, taps):
        tap(t)

    for b in range(batch):
        whole = pooled[b]
        for o in range(n):
            tpart[o, b] = whole[:, o * oblk : (o + 1) * oblk].astype(bf16)

    def t_copy(d):
        other = lax.rem(me + d, n)
        return remote(tpart.at[other], trunk_ref.at[:, pl.ds(pl.multiple_of(me * half, edge), half)],
                      t_send.at[d - 1], t_recv.at[d - 1], {"seq": other})

    for d in range(1, n):
        t_copy(d).start()
    trunk_ref[:, pl.ds(pl.multiple_of(me * half, edge), half), :] = tpart[me]

    def z_copy(t, d):
        other = lax.rem(zme + d, zs)
        return remote(zpart.at[t, other], zrecv.at[t, d - 1], z_send.at[t, d - 1],
                      z_recv.at[t, d - 1], {"dp": other})

    def collect(t):
        if square:
            for h in range(2):
                y_copy(t, h).wait_recv()
            total = own[t] + jnp.concatenate(
                [recv[t, h, 0].astype(f32) + recv2[t, h].astype(f32) for h in range(2)], axis=0)
        else:
            total = own[t]
            for d in range(firsts):
                x_copy(t, d).wait_recv()
            for d in range(firsts):
                total += recv[t, d].astype(f32)
        for q in range(zs):
            piece = total[:, q * iblk : (q + 1) * iblk]
            zown[t, q] = piece
            zpart[t, q] = piece.astype(bf16)
        for d in range(1, zs):
            z_copy(t, d).start()

    @pl.loop(0, chans // cols)
    def _(tile):
        c0 = pl.multiple_of(tile * cols, cols)
        q = [
            lax.dot_general(gext[...], w_ref[k, pl.ds(c0, cols), :], (((1,), (1,)), ((), ())),
                            preferred_element_type=f32)
            for k in range(taps)
        ]
        q01, q12, q23, q34 = q[0] + q[1], q[1] + q[2], q[2] + q[3], q[3] + q[4]
        for b in range(batch):
            at = slice(b * half, (b + 1) * half)
            even = q12[at] + sooner(q[0][at], b, q[0][rows:]) + later(q34[at], b, q34[rows:])
            odd = q23[at] + sooner(q01[at], b, q01[rows:]) + later(q[4][at], b, q[4][rows:])
            tslope[b, :, pl.ds(c0, cols)] = tslope[b, :, pl.ds(c0, cols)] * even
            tslope[b, :, pl.ds(chans + c0, cols)] = tslope[b, :, pl.ds(chans + c0, cols)] * odd

        @pl.when(tile < taps - tiles)
        def _():
            forward(tiles + tile)

        collect(tile)

    @pl.loop(0, batch * per)
    def _(step):
        b = step // per
        r = pl.multiple_of(lax.rem(step, per) * chunk, chunk)
        up = 0.5 * g_ref[b, pl.ds(r, chunk), :].astype(f32)
        for p in range(2):
            lanes = slice(p * chans, (p + 1) * chans)
            block = fd[b, pl.ds(r, chunk), lanes].astype(f32)
            scaled = tslope[b, pl.ds(r, chunk), lanes]
            inverse = lax.rsqrt(jnp.mean(block * block, axis=-1, keepdims=True) + epsilon)
            centred = jnp.mean(scaled * block, axis=-1, keepdims=True) * inverse * inverse
            result = up + scaled - block * centred
            for c in range(chans // 128):
                stage[c, pl.ds(p, chunk, stride=2), :] = result[:, c * 128 : (c + 1) * 128]
        mixed = jnp.concatenate([stage[c] for c in range(chans // 128)], axis=1)
        igrad_ref[b, pl.ds(pl.multiple_of(2 * r, chunk), 2 * chunk), :] = mixed.astype(bf16)

    @pl.loop(tiles, taps)
    def _(t):
        collect(t)

    @pl.loop(0, taps)
    def _(t):
        total = zown[t, zme]
        for d in range(1, zs):
            z_copy(t, d).wait_recv()
        for d in range(1, zs):
            total += zrecv[t, d - 1].astype(f32)
        wg_ref[t] = total
        for d in range(1, zs):
            z_copy(t, d).wait_send()
        for d in range(firsts):
            x_copy(t, d).wait_send()
        if square:
            for h in range(2):
                y_copy(t, h).wait_send()

    for d in range(1, n):
        t_copy(d).wait()
    for b in range(batch):
        sib_copy(b).wait_send()
    send_gt.wait_send()


def shards(features, weight, cotangent):
    n = lax.axis_size("seq")
    zs = lax.axis_size("dp")
    taps, _, chans = weight.shape
    batch, length, _ = features.shape
    half = length // 2
    rows = batch * half
    chips = n // 2
    oblk = chans // n
    iblk = chans // zs
    square = chips == 4
    hblk = oblk // 2
    firsts = 2 if square else chips - 1
    sends = (taps, 2, 2, hblk, chans) if square else (taps, chips, oblk, chans)
    lands = sends if square else (taps, chips - 1, oblk, chans)
    relay = (taps, 2, hblk, chans) if square else (1, 1, 16, 128)
    vmem = pl.BlockSpec(memory_space=pltpu.VMEM)
    dma = pltpu.SemaphoreType.DMA
    trunk, igrad, wg = pl.pallas_call(
        functools.partial(kernel, n, zs),
        out_shape=(
            jax.ShapeDtypeStruct((batch, half * n, oblk), bf16),
            jax.ShapeDtypeStruct((batch, length, chans), bf16),
            jax.ShapeDtypeStruct((taps, oblk, iblk), f32),
        ),
        in_specs=[vmem, pl.BlockSpec(memory_space=pl.ANY), vmem],
        out_specs=(vmem,) * 3,
        scratch_shapes=[
            pltpu.VMEM(weight.shape, bf16),
            pltpu.VMEM((batch, half, 2 * chans), bf16),
            pltpu.VMEM((chans // 128, 64, 128), f32),
            pltpu.VMEM((2, batch, edge, chans), bf16),
            pltpu.VMEM((2, batch, edge, chans), bf16),
            pltpu.VMEM((2, rows + edge, chans), bf16),
            pltpu.VMEM((2, rows, chans), bf16),
            pltpu.VMEM((rows + edge, chans), bf16),
            pltpu.VMEM((2, 3, batch, chips, oblk, half), bf16),
            pltpu.VMEM((3, batch, chips, oblk, half), bf16),
            pltpu.VMEM((batch, half, 2 * chans), f32),
            pltpu.VMEM((2, chips, oblk, chans), f32),
            pltpu.VMEM(sends, bf16),
            pltpu.VMEM(lands, bf16),
            pltpu.VMEM(relay, bf16),
            pltpu.VMEM(relay, bf16),
            pltpu.VMEM(relay, f32),
            pltpu.VMEM((taps, oblk, chans), f32),
            pltpu.VMEM((taps, zs, oblk, iblk), bf16),
            pltpu.VMEM((taps, zs - 1, oblk, iblk), bf16),
            pltpu.VMEM((taps, zs, oblk, iblk), f32),
            pltpu.VMEM((batch, half, chans), f32),
            pltpu.VMEM((n, batch, half, oblk), bf16),
            dma((1,)), dma((4,)), dma((4,)), dma((batch + 1,)), dma((batch + 1,)),
            dma((taps, firsts)), dma((taps, firsts)), dma((taps, 2)), dma((taps, 2)),
            dma((taps, zs - 1)), dma((taps, zs - 1)),
            dma((n - 1,)), dma((n - 1,)),
        ],
        compiler_params=pltpu.CompilerParams(
            collective_id=0, has_side_effects=True, vmem_limit_bytes=60 * 1024 * 1024
        ),
        cost_estimate=pl.CostEstimate(
            flops=2 * rows * chans * chans * 21, bytes_accessed=12_000_000, transcendentals=4 * rows * chans
        ),
    )(features, weight, cotangent)
    return trunk, igrad, jnp.swapaxes(wg, 1, 2)


def solution(mesh):
    return jax.shard_map(
        shards,
        mesh=mesh,
        in_specs=(P("dp", "seq", None), P(), P("dp", "seq", None)),
        out_specs=(P("dp", None, "seq"), P("dp", "seq", None), P(None, "dp", "seq")),
        check_vma=False,
    )
```

```python
import functools

import jax
import jax.numpy as jnp
from jax import lax
from jax.experimental import pallas as pl
from jax.experimental.pallas import tpu as pltpu
from jax.sharding import PartitionSpec as P

epsilon = 1e-06
root_half = 0.7071067811865476
inv_root_two_pi = 0.3989422804014327
edge = 16
f32 = jnp.float32
bf16 = jnp.bfloat16


def phases(rows):
    inverse = lax.rsqrt(jnp.mean(rows * rows, axis=-1, keepdims=True) + epsilon)
    normed = rows * inverse
    cdf = 0.5 * (1.0 + lax.erf(normed * root_half))
    slope = cdf + normed * inv_root_two_pi * jnp.exp(-0.5 * normed * normed)
    return normed * cdf, slope * inverse


def kernel(
    n, zs, f_ref, w_hbm, g_ref,
    trunk_ref, igrad_ref, wg_ref,
    w_ref, fd, stage, halo_f, halo_g, acts, gext, gt_all, gt_out, tslope, prod, part, recv, part2, recv2, keep, own,
    zpart, zrecv, zown, pooled, tpart, tland,
    w_sem, halo_send, halo_recv, sib_send, sib_recv, x_send, x_recv, y_send, y_recv, z_send, z_recv, t_send, t_recv,
):
    batch, length, chans = f_ref.shape
    half = length // 2
    taps = w_hbm.shape[0]
    rows = batch * half
    chips = n // 2
    oblk = chans // n
    iblk = chans // zs
    me = lax.axis_index("seq")
    core = lax.rem(me, 2)
    chip = me // 2
    sib = me + 1 - 2 * core
    zme = lax.axis_index("dp")

    load = pltpu.make_async_copy(w_hbm, w_ref, w_sem.at[0])
    load.start()
    barrier = pltpu.get_barrier_semaphore()
    for d in range(1, n):
        pl.semaphore_signal(barrier, inc=1, device_id={"seq": lax.rem(me + d, n)},
                            device_id_type=pl.DeviceIdType.MESH)
    for d in range(1, zs):
        pl.semaphore_signal(barrier, inc=1, device_id={"dp": lax.rem(zme + d, zs)},
                            device_id_type=pl.DeviceIdType.MESH)
    pl.semaphore_wait(barrier, n - 1 + zs - 1)

    def remote(src, dst, ssem, rsem, where):
        return pltpu.make_async_remote_copy(
            src_ref=src, dst_ref=dst, send_sem=ssem, recv_sem=rsem,
            device_id=where, device_id_type=pl.DeviceIdType.MESH)

    right = {"seq": lax.rem(me + 1, n)}
    left = {"seq": lax.rem(me + n - 1, n)}
    halos = []
    for side, (where, start_last) in enumerate(((right, True), (left, False))):
        start = half - edge if start_last else 0
        f_start = length - edge if start_last else 0
        halos.append(remote(f_ref.at[:, pl.ds(f_start, edge)], halo_f.at[side],
                            halo_send.at[2 * side], halo_recv.at[2 * side], where))
        halos.append(remote(g_ref.at[:, pl.ds(start, edge)], halo_g.at[side],
                            halo_send.at[2 * side + 1], halo_recv.at[2 * side + 1], where))
    for copy in halos:
        copy.start()

    chunk = 32
    per = half // chunk

    def activate(b):
        @pl.loop(0, per)
        def _(step):
            r = pl.multiple_of(step * chunk, chunk)
            raw = f_ref[b, pl.ds(pl.multiple_of(2 * r, chunk), 2 * chunk), :].astype(f32)
            for c in range(chans // 128):
                stage[c] = raw[:, c * 128 : (c + 1) * 128]
            for p in range(2):
                block = jnp.concatenate(
                    [stage[c, pl.ds(p, chunk, stride=2), :] for c in range(chans // 128)], axis=1)
                act, slope = phases(block)
                fd[b, pl.ds(r, chunk), p * chans : (p + 1) * chans] = block.astype(bf16)
                acts[p, pl.ds(pl.multiple_of(edge + b * half + r, edge), chunk), :] = act.astype(bf16)
                tslope[b, pl.ds(r, chunk), p * chans : (p + 1) * chans] = slope

    to_sib = {"seq": sib}

    def sib_copy(b):
        return remote(acts.at[:, pl.ds(edge + b * half, half)],
                      acts.at[:, pl.ds(edge + rows + b * half, half)], sib_send.at[b + 1], sib_recv.at[b + 1], to_sib)

    for b in range(batch - 1):
        activate(b)
        sib_copy(b).start()

    for copy in halos:
        copy.wait()
    index = lax.broadcasted_iota(jnp.int32, (edge, 1), 0)
    has_left = jnp.where(me > 0, 1.0, 0.0)
    has_right = jnp.where(me < n - 1, 1.0, 0.0)

    def edge_rows(ref, last, first):
        out = jnp.zeros((edge, chans), f32)
        for b in range(batch):
            low = ref[0, b].astype(f32)[last : last + 1, :] * has_left
            high = ref[1, b].astype(f32)[first : first + 1, :] * has_right
            out = jnp.where(index == b, low, out)
            out = jnp.where(index == batch + b, high, out)
        return out

    hg = 0.5 * edge_rows(halo_g, edge - 1, 0)
    gext[pl.ds(rows, edge), :] = hg.astype(bf16)

    spot = lax.broadcasted_iota(jnp.int32, (half, 1), 0)

    def later(block, b, tail):
        return jnp.where(spot == 0, tail[b : b + 1, :], pltpu.roll(block, 1, 0))

    def sooner(block, b, tail):
        return jnp.where(spot == half - 1, tail[batch + b : batch + b + 1, :],
                         pltpu.roll(block, half - 1, 0))

    shifted = ([], [], [])
    for b in range(batch):
        g0 = 0.5 * g_ref[b].astype(f32)
        gext[pl.ds(b * half, half), :] = g0.astype(bf16)
        for s, block in enumerate((sooner(g0, b, hg), g0, later(g0, b, hg))):
            shifted[s].append(block)
    for s in range(3):
        turned = jnp.concatenate(shifted[s], axis=0).T.astype(bf16)
        for m in range(chips):
            low = turned[2 * m * oblk : (2 * m + 1) * oblk, :]
            high = turned[(2 * m + 1) * oblk : (2 * m + 2) * oblk, :]
            gt_all[s, m * oblk : (m + 1) * oblk, 0:rows] = jnp.where(core == 0, low, high)
            gt_out[s, m * oblk : (m + 1) * oblk, :] = jnp.where(core == 0, high, low)
    send_gt = remote(gt_out, gt_all.at[:, :, pl.ds(rows, rows)], sib_send.at[0], sib_recv.at[0], to_sib)
    send_gt.start()
    activate(batch - 1)
    sib_copy(batch - 1).start()
    for p in range(2):
        act, _ = phases(edge_rows(halo_f, edge - 2 + p, p))
        acts[p, pl.ds(0, edge), :] = act.astype(bf16)
    send_gt.wait_recv()
    for b in range(batch):
        sib_copy(b).wait_recv()

    def product(s, p, slot):
        total = jnp.dot(gt_all[s], acts[p, edge : edge + 2 * rows, :], preferred_element_type=f32)
        for m in range(chips):
            prod[slot, m] = total[m * oblk : (m + 1) * oblk, :]

    square = chips == 4
    hblk = oblk // 2
    x = lax.rem(chip, 2)
    y = chip // 2
    beside = chip + 1 - 2 * x
    beyond = chip + 2 - 4 * y
    across = beside + 2 - 4 * y
    near = ((beside, slice(0, hblk)), (beyond, slice(hblk, oblk)))

    def x_copy(t, d):
        if square:
            return remote(part.at[t, d], recv.at[t, d], x_send.at[t, d], x_recv.at[t, d],
                          {"seq": 2 * near[d][0] + core})
        other = lax.rem(chip + d + 1, chips)
        return remote(part.at[t, other], recv.at[t, d], x_send.at[t, d],
                      x_recv.at[t, d], {"seq": 2 * other + core})

    def y_copy(t, h):
        return remote(part2.at[t, h], recv2.at[t, h], y_send.at[t, h], y_recv.at[t, h],
                      {"seq": 2 * near[1 - h][0] + core})

    firsts = 2 if square else chips - 1

    def tap(t):
        product((t + 1) // 2, lax.rem(t + 1, 2), lax.rem(t + 1, 2))

        def both(m, at=slice(None)):
            return prod[0, m, at] + prod[1, m, at]

        if square:
            for h in range(2):
                at = near[h][1]
                part[t, h, 0] = both(near[h][0], at).astype(bf16)
                part[t, h, 1] = both(across, at).astype(bf16)
                keep[t, h] = both(near[1 - h][0], at)
        else:
            for m in range(chips):
                part[t, m] = both(m).astype(bf16)
        for d in range(firsts):
            x_copy(t, d).start()
        own[t] = both(chip)

    def forward(t):
        if square:
            for h in range(2):
                x_copy(t, h).wait_recv()
                part2[t, h] = (keep[t, h] + recv[t, h, 1].astype(f32)).astype(bf16)
                y_copy(t, h).start()

    product(0, 0, 0)
    tap(0)
    load.wait()

    cols = 256

    @pl.loop(0, chans // cols)
    def _(tile):
        tap(tile + 1)
        c0 = pl.multiple_of(tile * cols, cols)
        w = [w_ref[k, :, pl.ds(c0, cols)] for k in range(taps)]

        def dots(pairs):
            total = None
            for p, k in pairs:
                one = jnp.dot(acts[p, 0 : edge + rows, :], w[k], preferred_element_type=f32)
                total = one if total is None else total + one
            return total

        before = dots(((0, 0), (1, 0), (1, 1)))
        middle = dots(((0, 1), (0, 2), (1, 2), (1, 3)))
        after = dots(((0, 3), (0, 4), (1, 4)))
        for b in range(batch):
            at = slice(edge + b * half, edge + (b + 1) * half)
            total = middle[at] + later(before[at], b, before[:edge]) + sooner(after[at], b, after[:edge])
            total += fd[b, :, pl.ds(c0, cols)].astype(f32)
            total += fd[b, :, pl.ds(chans + c0, cols)].astype(f32)
            pooled[b * half : (b + 1) * half, pl.ds(c0, cols)] = 0.5 * total
        forward(tile)

    tiles = chans // cols
    for t in range(tiles + 1, taps):
        tap(t)

    turned = pooled[...].T.astype(bf16)
    for o in range(n):
        tpart[o] = turned[o * oblk : (o + 1) * oblk, :]

    def t_copy(d):
        other = lax.rem(me + d, n)
        return remote(tpart.at[other], tland.at[me],
                      t_send.at[d - 1], t_recv.at[d - 1], {"seq": other})

    for d in range(1, n):
        t_copy(d).start()
    tland[me] = tpart[me]

    def z_copy(t, d):
        other = lax.rem(zme + d, zs)
        return remote(zpart.at[t, other], zrecv.at[t, d - 1], z_send.at[t, d - 1],
                      z_recv.at[t, d - 1], {"dp": other})

    def collect(t):
        if square:
            for h in range(2):
                y_copy(t, h).wait_recv()
            total = own[t] + jnp.concatenate(
                [recv[t, h, 0].astype(f32) + recv2[t, h].astype(f32) for h in range(2)], axis=0)
        else:
            total = own[t]
            for d in range(firsts):
                x_copy(t, d).wait_recv()
            for d in range(firsts):
                total += recv[t, d].astype(f32)
        for q in range(zs):
            piece = total[:, q * iblk : (q + 1) * iblk]
            zown[t, q] = piece
            zpart[t, q] = piece.astype(bf16)
        for d in range(1, zs):
            z_copy(t, d).start()

    @pl.loop(0, chans // cols)
    def _(tile):
        c0 = pl.multiple_of(tile * cols, cols)
        q = [
            lax.dot_general(gext[...], w_ref[k, pl.ds(c0, cols), :], (((1,), (1,)), ((), ())),
                            preferred_element_type=f32)
            for k in range(taps)
        ]
        q01, q12, q23, q34 = q[0] + q[1], q[1] + q[2], q[2] + q[3], q[3] + q[4]
        for b in range(batch):
            at = slice(b * half, (b + 1) * half)
            even = q12[at] + sooner(q[0][at], b, q[0][rows:]) + later(q34[at], b, q34[rows:])
            odd = q23[at] + sooner(q01[at], b, q01[rows:]) + later(q[4][at], b, q[4][rows:])
            tslope[b, :, pl.ds(c0, cols)] = tslope[b, :, pl.ds(c0, cols)] * even
            tslope[b, :, pl.ds(chans + c0, cols)] = tslope[b, :, pl.ds(chans + c0, cols)] * odd

        @pl.when(tile < taps - tiles)
        def _():
            forward(tiles + tile)

        collect(tile)

    @pl.loop(0, batch * per)
    def _(step):
        b = step // per
        r = pl.multiple_of(lax.rem(step, per) * chunk, chunk)
        up = 0.5 * g_ref[b, pl.ds(r, chunk), :].astype(f32)
        for p in range(2):
            lanes = slice(p * chans, (p + 1) * chans)
            block = fd[b, pl.ds(r, chunk), lanes].astype(f32)
            scaled = tslope[b, pl.ds(r, chunk), lanes]
            inverse = lax.rsqrt(jnp.mean(block * block, axis=-1, keepdims=True) + epsilon)
            centred = jnp.mean(scaled * block, axis=-1, keepdims=True) * inverse * inverse
            result = up + scaled - block * centred
            for c in range(chans // 128):
                stage[c, pl.ds(p, chunk, stride=2), :] = result[:, c * 128 : (c + 1) * 128]
        mixed = jnp.concatenate([stage[c] for c in range(chans // 128)], axis=1)
        igrad_ref[b, pl.ds(pl.multiple_of(2 * r, chunk), 2 * chunk), :] = mixed.astype(bf16)

    @pl.loop(tiles, taps)
    def _(t):
        collect(t)

    for d in range(1, n):
        t_copy(d).wait()
    for o in range(n):
        for b in range(batch):
            trunk_ref[b, :, o * half : (o + 1) * half] = tland[o, :, b * half : (b + 1) * half]

    @pl.loop(0, taps)
    def _(t):
        total = zown[t, zme]
        for d in range(1, zs):
            z_copy(t, d).wait_recv()
        for d in range(1, zs):
            total += zrecv[t, d - 1].astype(f32)
        wg_ref[t] = total
        for d in range(1, zs):
            z_copy(t, d).wait_send()
        for d in range(firsts):
            x_copy(t, d).wait_send()
        if square:
            for h in range(2):
                y_copy(t, h).wait_send()

    for b in range(batch):
        sib_copy(b).wait_send()
    send_gt.wait_send()


def shards(features, weight, cotangent):
    n = lax.axis_size("seq")
    zs = lax.axis_size("dp")
    taps, _, chans = weight.shape
    batch, length, _ = features.shape
    half = length // 2
    rows = batch * half
    chips = n // 2
    oblk = chans // n
    iblk = chans // zs
    square = chips == 4
    hblk = oblk // 2
    firsts = 2 if square else chips - 1
    sends = (taps, 2, 2, hblk, chans) if square else (taps, chips, oblk, chans)
    lands = sends if square else (taps, chips - 1, oblk, chans)
    relay = (taps, 2, hblk, chans) if square else (1, 1, 16, 128)
    vmem = pl.BlockSpec(memory_space=pltpu.VMEM)
    dma = pltpu.SemaphoreType.DMA
    trunk, igrad, wg = pl.pallas_call(
        functools.partial(kernel, n, zs),
        out_shape=(
            jax.ShapeDtypeStruct((batch, oblk, half * n), bf16),
            jax.ShapeDtypeStruct((batch, length, chans), bf16),
            jax.ShapeDtypeStruct((taps, oblk, iblk), f32),
        ),
        in_specs=[vmem, pl.BlockSpec(memory_space=pl.ANY), vmem],
        out_specs=(vmem,) * 3,
        scratch_shapes=[
            pltpu.VMEM(weight.shape, bf16),
            pltpu.VMEM((batch, half, 2 * chans), bf16),
            pltpu.VMEM((chans // 128, 64, 128), f32),
            pltpu.VMEM((2, batch, edge, chans), bf16),
            pltpu.VMEM((2, batch, edge, chans), bf16),
            pltpu.VMEM((2, edge + 2 * rows, chans), bf16),
            pltpu.VMEM((rows + edge, chans), bf16),
            pltpu.VMEM((3, chips * oblk, 2 * rows), bf16),
            pltpu.VMEM((3, chips * oblk, rows), bf16),
            pltpu.VMEM((batch, half, 2 * chans), f32),
            pltpu.VMEM((2, chips, oblk, chans), f32),
            pltpu.VMEM(sends, bf16),
            pltpu.VMEM(lands, bf16),
            pltpu.VMEM(relay, bf16),
            pltpu.VMEM(relay, bf16),
            pltpu.VMEM(relay, f32),
            pltpu.VMEM((taps, oblk, chans), f32),
            pltpu.VMEM((taps, zs, oblk, iblk), bf16),
            pltpu.VMEM((taps, zs - 1, oblk, iblk), bf16),
            pltpu.VMEM((taps, zs, oblk, iblk), f32),
            pltpu.VMEM((rows, chans), f32),
            pltpu.VMEM((n, oblk, rows), bf16),
            pltpu.VMEM((n, oblk, rows), bf16),
            dma((1,)), dma((4,)), dma((4,)), dma((batch + 1,)), dma((batch + 1,)),
            dma((taps, firsts)), dma((taps, firsts)), dma((taps, 2)), dma((taps, 2)),
            dma((taps, zs - 1)), dma((taps, zs - 1)),
            dma((n - 1,)), dma((n - 1,)),
        ],
        compiler_params=pltpu.CompilerParams(
            collective_id=0, has_side_effects=True, vmem_limit_bytes=60 * 1024 * 1024
        ),
        cost_estimate=pl.CostEstimate(
            flops=2 * rows * chans * chans * 21, bytes_accessed=12_000_000, transcendentals=4 * rows * chans
        ),
    )(features, weight, cotangent)
    return jnp.swapaxes(trunk, 1, 2), igrad, jnp.swapaxes(wg, 1, 2)


def solution(mesh):
    return jax.shard_map(
        shards,
        mesh=mesh,
        in_specs=(P("dp", "seq", None), P(), P("dp", "seq", None)),
        out_specs=(P("dp", None, "seq"), P("dp", "seq", None), P(None, "dp", "seq")),
        check_vma=False,
    )
```

```python
import functools

import jax
import jax.numpy as jnp
from jax import lax
from jax.experimental import pallas as pl
from jax.experimental.pallas import tpu as pltpu
from jax.sharding import PartitionSpec as P

epsilon = 1e-06
root_half = 0.7071067811865476
inv_root_two_pi = 0.3989422804014327
edge = 16
f32 = jnp.float32
bf16 = jnp.bfloat16


def phases(rows):
    inverse = lax.rsqrt(jnp.mean(rows * rows, axis=-1, keepdims=True) + epsilon)
    normed = rows * inverse
    cdf = 0.5 * (1.0 + lax.erf(normed * root_half))
    slope = cdf + normed * inv_root_two_pi * jnp.exp(-0.5 * normed * normed)
    return normed * cdf, slope * inverse


def kernel(
    n, zs, f_ref, w_hbm, g_ref,
    trunk_ref, igrad_ref, wg_ref,
    w_ref, fd, stage, halo_f, halo_g, acts, gext, gt_all, gt_out, tslope, prod, part, recv, part2, recv2, keep, own,
    zpart, zrecv, zown, pooled, tpart, tland,
    w_sem, halo_send, halo_recv, sib_send, sib_recv, x_send, x_recv, y_send, y_recv, z_send, z_recv, t_send, t_recv,
):
    batch, length, chans = f_ref.shape
    half = length // 2
    taps = w_hbm.shape[0]
    rows = batch * half
    chips = n // 2
    oblk = chans // n
    iblk = chans // zs
    me = lax.axis_index("seq")
    core = lax.rem(me, 2)
    chip = me // 2
    sib = me + 1 - 2 * core
    zme = lax.axis_index("dp")

    load = pltpu.make_async_copy(w_hbm, w_ref, w_sem.at[0])
    load.start()
    barrier = pltpu.get_barrier_semaphore()
    for d in range(1, n):
        pl.semaphore_signal(barrier, inc=1, device_id={"seq": lax.rem(me + d, n)},
                            device_id_type=pl.DeviceIdType.MESH)
    for d in range(1, zs):
        pl.semaphore_signal(barrier, inc=1, device_id={"dp": lax.rem(zme + d, zs)},
                            device_id_type=pl.DeviceIdType.MESH)

    def remote(src, dst, ssem, rsem, where):
        return pltpu.make_async_remote_copy(
            src_ref=src, dst_ref=dst, send_sem=ssem, recv_sem=rsem,
            device_id=where, device_id_type=pl.DeviceIdType.MESH)

    right = {"seq": lax.rem(me + 1, n)}
    left = {"seq": lax.rem(me + n - 1, n)}
    halos = []
    for side, (where, start_last) in enumerate(((right, True), (left, False))):
        start = half - edge if start_last else 0
        f_start = length - edge if start_last else 0
        halos.append(remote(f_ref.at[:, pl.ds(f_start, edge)], halo_f.at[side],
                            halo_send.at[2 * side], halo_recv.at[2 * side], where))
        halos.append(remote(g_ref.at[:, pl.ds(start, edge)], halo_g.at[side],
                            halo_send.at[2 * side + 1], halo_recv.at[2 * side + 1], where))

    chunk = 32
    per = half // chunk

    def activate(b):
        @pl.loop(0, per)
        def _(step):
            r = pl.multiple_of(step * chunk, chunk)
            raw = f_ref[b, pl.ds(pl.multiple_of(2 * r, chunk), 2 * chunk), :].astype(f32)
            for c in range(chans // 128):
                stage[c] = raw[:, c * 128 : (c + 1) * 128]
            for p in range(2):
                block = jnp.concatenate(
                    [stage[c, pl.ds(p, chunk, stride=2), :] for c in range(chans // 128)], axis=1)
                act, slope = phases(block)
                fd[b, pl.ds(r, chunk), p * chans : (p + 1) * chans] = block.astype(bf16)
                acts[p, pl.ds(pl.multiple_of(edge + b * half + r, edge), chunk), :] = act.astype(bf16)
                tslope[b, pl.ds(r, chunk), p * chans : (p + 1) * chans] = slope

    to_sib = {"seq": sib}

    def sib_copy(b):
        return remote(acts.at[:, pl.ds(edge + b * half, half)],
                      acts.at[:, pl.ds(edge + rows + b * half, half)], sib_send.at[b + 1], sib_recv.at[b + 1], to_sib)

    activate(0)
    pl.semaphore_wait(barrier, n - 1 + zs - 1)
    for copy in halos:
        copy.start()
    sib_copy(0).start()
    for b in range(1, batch):
        activate(b)
        sib_copy(b).start()

    for copy in halos:
        copy.wait()
    index = lax.broadcasted_iota(jnp.int32, (edge, 1), 0)
    has_left = jnp.where(me > 0, 1.0, 0.0)
    has_right = jnp.where(me < n - 1, 1.0, 0.0)

    def edge_rows(ref, last, first):
        out = jnp.zeros((edge, chans), f32)
        for b in range(batch):
            low = ref[0, b].astype(f32)[last : last + 1, :] * has_left
            high = ref[1, b].astype(f32)[first : first + 1, :] * has_right
            out = jnp.where(index == b, low, out)
            out = jnp.where(index == batch + b, high, out)
        return out

    hg = 0.5 * edge_rows(halo_g, edge - 1, 0)
    gext[pl.ds(rows, edge), :] = hg.astype(bf16)

    spot = lax.broadcasted_iota(jnp.int32, (half, 1), 0)

    def later(block, b, tail):
        return jnp.where(spot == 0, tail[b : b + 1, :], pltpu.roll(block, 1, 0))

    def sooner(block, b, tail):
        return jnp.where(spot == half - 1, tail[batch + b : batch + b + 1, :],
                         pltpu.roll(block, half - 1, 0))

    shifted = ([], [], [])
    for b in range(batch):
        g0 = 0.5 * g_ref[b].astype(f32)
        gext[pl.ds(b * half, half), :] = g0.astype(bf16)
        for s, block in enumerate((sooner(g0, b, hg), g0, later(g0, b, hg))):
            shifted[s].append(block)
    for s in range(3):
        turned = jnp.concatenate(shifted[s], axis=0).T.astype(bf16)
        for m in range(chips):
            low = turned[2 * m * oblk : (2 * m + 1) * oblk, :]
            high = turned[(2 * m + 1) * oblk : (2 * m + 2) * oblk, :]
            gt_all[s, m * oblk : (m + 1) * oblk, 0:rows] = jnp.where(core == 0, low, high)
            gt_out[s, m * oblk : (m + 1) * oblk, :] = jnp.where(core == 0, high, low)
    send_gt = remote(gt_out, gt_all.at[:, :, pl.ds(rows, rows)], sib_send.at[0], sib_recv.at[0], to_sib)
    send_gt.start()
    for p in range(2):
        act, _ = phases(edge_rows(halo_f, edge - 2 + p, p))
        acts[p, pl.ds(0, edge), :] = act.astype(bf16)
    send_gt.wait_recv()
    for b in range(batch):
        sib_copy(b).wait_recv()

    def product(s, p, slot):
        total = jnp.dot(gt_all[s], acts[p, edge : edge + 2 * rows, :], preferred_element_type=f32)
        for m in range(chips):
            prod[slot, m] = total[m * oblk : (m + 1) * oblk, :]

    square = chips == 4
    hblk = oblk // 2
    x = lax.rem(chip, 2)
    y = chip // 2
    beside = chip + 1 - 2 * x
    beyond = chip + 2 - 4 * y
    across = beside + 2 - 4 * y
    near = ((beside, slice(0, hblk)), (beyond, slice(hblk, oblk)))

    def x_copy(t, d):
        if square:
            return remote(part.at[t, d], recv.at[t, d], x_send.at[t, d], x_recv.at[t, d],
                          {"seq": 2 * near[d][0] + core})
        other = lax.rem(chip + d + 1, chips)
        return remote(part.at[t, other], recv.at[t, d], x_send.at[t, d],
                      x_recv.at[t, d], {"seq": 2 * other + core})

    def y_copy(t, h):
        return remote(part2.at[t, h], recv2.at[t, h], y_send.at[t, h], y_recv.at[t, h],
                      {"seq": 2 * near[1 - h][0] + core})

    firsts = 2 if square else chips - 1

    def tap(t):
        product((t + 1) // 2, lax.rem(t + 1, 2), lax.rem(t + 1, 2))

        def both(m, at=slice(None)):
            return prod[0, m, at] + prod[1, m, at]

        if square:
            for h in range(2):
                at = near[h][1]
                part[t, h, 0] = both(near[h][0], at).astype(bf16)
                part[t, h, 1] = both(across, at).astype(bf16)
                keep[t, h] = both(near[1 - h][0], at)
        else:
            for m in range(chips):
                part[t, m] = both(m).astype(bf16)
        for d in range(firsts):
            x_copy(t, d).start()
        own[t] = both(chip)

    def forward(t):
        if square:
            for h in range(2):
                x_copy(t, h).wait_recv()
                part2[t, h] = (keep[t, h] + recv[t, h, 1].astype(f32)).astype(bf16)
                y_copy(t, h).start()

    product(0, 0, 0)
    tap(0)
    load.wait()

    cols = 256

    @pl.loop(0, chans // cols)
    def _(tile):
        tap(tile + 1)
        c0 = pl.multiple_of(tile * cols, cols)
        w = [w_ref[k, :, pl.ds(c0, cols)] for k in range(taps)]

        def dots(pairs):
            total = None
            for p, k in pairs:
                one = jnp.dot(acts[p, 0 : edge + rows, :], w[k], preferred_element_type=f32)
                total = one if total is None else total + one
            return total

        before = dots(((0, 0), (1, 0), (1, 1)))
        middle = dots(((0, 1), (0, 2), (1, 2), (1, 3)))
        after = dots(((0, 3), (0, 4), (1, 4)))
        for b in range(batch):
            at = slice(edge + b * half, edge + (b + 1) * half)
            total = middle[at] + later(before[at], b, before[:edge]) + sooner(after[at], b, after[:edge])
            total += fd[b, :, pl.ds(c0, cols)].astype(f32)
            total += fd[b, :, pl.ds(chans + c0, cols)].astype(f32)
            pooled[b * half : (b + 1) * half, pl.ds(c0, cols)] = 0.5 * total
        forward(tile)

    tiles = chans // cols
    for t in range(tiles + 1, taps):
        tap(t)

    turned = pooled[...].T.astype(bf16)
    for o in range(n):
        tpart[o] = turned[o * oblk : (o + 1) * oblk, :]

    def t_copy(d):
        other = lax.rem(me + d, n)
        return remote(tpart.at[other], tland.at[me],
                      t_send.at[d - 1], t_recv.at[d - 1], {"seq": other})

    for d in range(1, n):
        t_copy(d).start()
    tland[me] = tpart[me]

    def z_copy(t, d):
        other = lax.rem(zme + d, zs)
        return remote(zpart.at[t, other], zrecv.at[t, d - 1], z_send.at[t, d - 1],
                      z_recv.at[t, d - 1], {"dp": other})

    def collect(t):
        if square:
            for h in range(2):
                y_copy(t, h).wait_recv()
            total = own[t] + jnp.concatenate(
                [recv[t, h, 0].astype(f32) + recv2[t, h].astype(f32) for h in range(2)], axis=0)
        else:
            total = own[t]
            for d in range(firsts):
                x_copy(t, d).wait_recv()
            for d in range(firsts):
                total += recv[t, d].astype(f32)
        for q in range(zs):
            piece = total[:, q * iblk : (q + 1) * iblk]
            zown[t, q] = piece
            zpart[t, q] = piece.astype(bf16)
        for d in range(1, zs):
            z_copy(t, d).start()

    @pl.loop(0, chans // cols)
    def _(tile):
        c0 = pl.multiple_of(tile * cols, cols)
        q = [
            lax.dot_general(gext[...], w_ref[k, pl.ds(c0, cols), :], (((1,), (1,)), ((), ())),
                            preferred_element_type=f32)
            for k in range(taps)
        ]
        q01, q12, q23, q34 = q[0] + q[1], q[1] + q[2], q[2] + q[3], q[3] + q[4]
        for b in range(batch):
            at = slice(b * half, (b + 1) * half)
            even = q12[at] + sooner(q[0][at], b, q[0][rows:]) + later(q34[at], b, q34[rows:])
            odd = q23[at] + sooner(q01[at], b, q01[rows:]) + later(q[4][at], b, q[4][rows:])
            tslope[b, :, pl.ds(c0, cols)] = tslope[b, :, pl.ds(c0, cols)] * even
            tslope[b, :, pl.ds(chans + c0, cols)] = tslope[b, :, pl.ds(chans + c0, cols)] * odd

        @pl.when(tile < taps - tiles)
        def _():
            forward(tiles + tile)

        collect(tile)

    @pl.loop(0, batch * per)
    def _(step):
        b = step // per
        r = pl.multiple_of(lax.rem(step, per) * chunk, chunk)
        up = 0.5 * g_ref[b, pl.ds(r, chunk), :].astype(f32)
        for p in range(2):
            lanes = slice(p * chans, (p + 1) * chans)
            block = fd[b, pl.ds(r, chunk), lanes].astype(f32)
            scaled = tslope[b, pl.ds(r, chunk), lanes]
            inverse = lax.rsqrt(jnp.mean(block * block, axis=-1, keepdims=True) + epsilon)
            centred = jnp.mean(scaled * block, axis=-1, keepdims=True) * inverse * inverse
            result = up + scaled - block * centred
            for c in range(chans // 128):
                stage[c, pl.ds(p, chunk, stride=2), :] = result[:, c * 128 : (c + 1) * 128]
        mixed = jnp.concatenate([stage[c] for c in range(chans // 128)], axis=1)
        igrad_ref[b, pl.ds(pl.multiple_of(2 * r, chunk), 2 * chunk), :] = mixed.astype(bf16)

    @pl.loop(tiles, taps)
    def _(t):
        collect(t)

    for d in range(1, n):
        t_copy(d).wait()
    for o in range(n):
        for b in range(batch):
            trunk_ref[b, :, o * half : (o + 1) * half] = tland[o, :, b * half : (b + 1) * half]

    @pl.loop(0, taps)
    def _(t):
        total = zown[t, zme]
        for d in range(1, zs):
            z_copy(t, d).wait_recv()
        for d in range(1, zs):
            total += zrecv[t, d - 1].astype(f32)
        wg_ref[t] = total.T
        for d in range(1, zs):
            z_copy(t, d).wait_send()
        for d in range(firsts):
            x_copy(t, d).wait_send()
        if square:
            for h in range(2):
                y_copy(t, h).wait_send()

    for b in range(batch):
        sib_copy(b).wait_send()
    send_gt.wait_send()


def shards(features, weight, cotangent):
    n = lax.axis_size("seq")
    zs = lax.axis_size("dp")
    taps, _, chans = weight.shape
    batch, length, _ = features.shape
    half = length // 2
    rows = batch * half
    chips = n // 2
    oblk = chans // n
    iblk = chans // zs
    square = chips == 4
    hblk = oblk // 2
    firsts = 2 if square else chips - 1
    sends = (taps, 2, 2, hblk, chans) if square else (taps, chips, oblk, chans)
    lands = sends if square else (taps, chips - 1, oblk, chans)
    relay = (taps, 2, hblk, chans) if square else (1, 1, 16, 128)
    vmem = pl.BlockSpec(memory_space=pltpu.VMEM)
    dma = pltpu.SemaphoreType.DMA
    trunk, igrad, wg = pl.pallas_call(
        functools.partial(kernel, n, zs),
        out_shape=(
            jax.ShapeDtypeStruct((batch, oblk, half * n), bf16),
            jax.ShapeDtypeStruct((batch, length, chans), bf16),
            jax.ShapeDtypeStruct((taps, iblk, oblk), f32),
        ),
        in_specs=[vmem, pl.BlockSpec(memory_space=pl.ANY), vmem],
        out_specs=(vmem,) * 3,
        scratch_shapes=[
            pltpu.VMEM(weight.shape, bf16),
            pltpu.VMEM((batch, half, 2 * chans), bf16),
            pltpu.VMEM((chans // 128, 64, 128), f32),
            pltpu.VMEM((2, batch, edge, chans), bf16),
            pltpu.VMEM((2, batch, edge, chans), bf16),
            pltpu.VMEM((2, edge + 2 * rows, chans), bf16),
            pltpu.VMEM((rows + edge, chans), bf16),
            pltpu.VMEM((3, chips * oblk, 2 * rows), bf16),
            pltpu.VMEM((3, chips * oblk, rows), bf16),
            pltpu.VMEM((batch, half, 2 * chans), f32),
            pltpu.VMEM((2, chips, oblk, chans), f32),
            pltpu.VMEM(sends, bf16),
            pltpu.VMEM(lands, bf16),
            pltpu.VMEM(relay, bf16),
            pltpu.VMEM(relay, bf16),
            pltpu.VMEM(relay, f32),
            pltpu.VMEM((taps, oblk, chans), f32),
            pltpu.VMEM((taps, zs, oblk, iblk), bf16),
            pltpu.VMEM((taps, zs - 1, oblk, iblk), bf16),
            pltpu.VMEM((taps, zs, oblk, iblk), f32),
            pltpu.VMEM((rows, chans), f32),
            pltpu.VMEM((n, oblk, rows), bf16),
            pltpu.VMEM((n, oblk, rows), bf16),
            dma((1,)), dma((4,)), dma((4,)), dma((batch + 1,)), dma((batch + 1,)),
            dma((taps, firsts)), dma((taps, firsts)), dma((taps, 2)), dma((taps, 2)),
            dma((taps, zs - 1)), dma((taps, zs - 1)),
            dma((n - 1,)), dma((n - 1,)),
        ],
        compiler_params=pltpu.CompilerParams(
            collective_id=0, has_side_effects=True, vmem_limit_bytes=60 * 1024 * 1024
        ),
        cost_estimate=pl.CostEstimate(
            flops=2 * rows * chans * chans * 21, bytes_accessed=12_000_000, transcendentals=4 * rows * chans
        ),
    )(features, weight, cotangent)
    return jnp.swapaxes(trunk, 1, 2), igrad, wg


def solution(mesh):
    return jax.shard_map(
        shards,
        mesh=mesh,
        in_specs=(P("dp", "seq", None), P(), P("dp", "seq", None)),
        out_specs=(P("dp", None, "seq"), P("dp", "seq", None), P(None, "dp", "seq")),
        check_vma=False,
    )
```
